256 devices in a mesh: seq: 4 (over x), expert: 64 (over z, y, core).
Axes of the slice: x: 4, y: 4, z: 8, core: 2. Of those that a mesh axis runs over, the one named last changes fastest.
Arguments:
- hidden_in: bfloat16 [2048, 4096], P(('seq', 'expert')), may hold values from -6 to 6
- w_query: bfloat16 [4096, 8192], P(None, 'expert'), may hold values from -0.09375 to 0.09375
- w_keyvalue: bfloat16 [4096, 1024], P(None, 'expert'), may hold values from -0.09375 to 0.09375
- w_out: bfloat16 [8192, 4096], P('expert'), may hold values from -0.5 to 0.5
- key_gain: float32 [128], replicated, may hold values from 0.1 to 1.9
- router: bfloat16 [4096, 64], replicated, may hold values from -0.03125 to 0.03125
- trainer_gate_up: bfloat16 [64, 4096, 2, 1024], P(None, 'expert', None, 'seq'), may hold values from -0.25 to 0.25
- trainer_down: bfloat16 [64, 1024, 4096], P(None, 'expert', 'seq'), may hold values from -1.5 to 1.5
- expert_ids: int32 [2048, 8], P(('seq', 'expert')), may hold values from 0 to 63, all different within a row; in each aligned block of 8 rows (0 to 7, 8 to 15, ...) at most 2 rows name the same one
- seq_lengths: int32 [3], replicated, may hold values from 1 to 1536, 2048 in all
- seq_offsets: int32 [3], replicated, may hold values from 0 to 4096
Outputs:
- mixed: bfloat16 [2048, 4096], P(('seq', 'expert'))
- kv_cache: bfloat16 [1024, 2048], P('expert', 'seq')
The draws below stay inside these ranges and needn't reach their ends.
Inputs may be any that keep to these rules, and one draw needn't show every extreme that they name: `expert_ids`: each row names 8 different experts; within the 8 rows of one device no expert is named more than 2 times, and in some device exactly 2 times. `seq_lengths`: the lengths sum to 2048; sequences lie end to end in this order; the longest is exactly the maximum.
All inputs are finite; a program needn't handle non-finite values.
Results may differ from the reference program's by a relative error of at most 0.025.
Values may be sent and summed in bfloat16 or wider, within the bound.
No kernel may reach another device: no remote copies, remote signals or barrier semaphores. Data moves between devices by JAX's collectives and lax.ppermute only.
A program may use at most 128 MiB of HBM per device.

```python
import math
import jax
import jax.numpy as jnp
import numpy as np
from jax import lax

D = 4096
HEADS = 64
KV_HEADS = 4
HEAD_DIM = 128
EXPERTS = 64
FFE = 1024
TOP = 8
NSEQ = 3
TOK_DEV = 8
CAP = 2
TOKENS = 2048
N_SEQ = 4
N_EXPERT = 64


def strengthened(entries, own_key, source, target, shards_of, factor):
    def block_of(axis_at):
        return (jnp.arange(entries.shape[axis_at]) // (entries.shape[axis_at] // shards_of)).reshape((-1,) + (1,) * (entries.ndim - 1 - axis_at))

    one_side = jax.random.permutation(own_key, shards_of)[block_of(target)]
    other_side = (block_of(target) + shards_of // 2) % shards_of
    return jnp.where((block_of(source) == one_side) | (block_of(source) == other_side), factor * entries, entries)


def steps_of(own_key, shape, split, smallest, high):
    def one(dim, blocks):
        heights = jax.random.uniform(jax.random.fold_in(jax.random.fold_in(own_key, 6), dim), (blocks,), jnp.float32, smallest / len(split), high / len(split))
        return jnp.repeat(jnp.exp(heights), shape[dim] // blocks).reshape((-1,) + (1,) * (len(shape) - dim - 1))

    gain = one(*split[0])
    for cut in split[1:]:
        gain = gain * one(*cut)
    return gain


def length_profile(amount, total, limit, slope):
    weights = [(1 << 20) // math.isqrt(standing ** slope) + 1 for standing in range(2, amount + 1)]
    spare, given = total - limit - (amount - 1), [1] * (amount - 1)
    while spare > 0:
        free = [i for i in range(amount - 1) if given[i] < limit]
        mass, budget = sum([weights[i] for i in free]), spare
        for i in free:
            addition = min(limit - given[i], max(1, budget * weights[i] // mass), spare)
            given[i] = given[i] + addition
            spare = spare - addition
    return np.array([limit] + given)


def ragged(rng, number_of, total, reach, skew):
    if number_of == 2:
        one = jax.random.randint(rng, (), max(1, total - reach), min(reach, total - 1) + 1)
        return jnp.stack([one, total - one])
    lengths = jnp.asarray(length_profile(number_of, total, reach, skew), jnp.int32)
    pairs = (number_of - 1) // 2
    donor, receiver = lengths[1:1 + 2 * pairs:2], lengths[2:2 + 2 * pairs:2]
    margin = jnp.minimum(donor - 1, reach - receiver)
    passed = jax.random.randint(jax.random.fold_in(rng, 1), (pairs,), 0, 1 << 20) % (margin + 1)
    lengths = lengths.at[1:1 + 2 * pairs:2].set(donor - passed).at[2:2 + 2 * pairs:2].set(receiver + passed)
    return lengths[jax.random.permutation(jax.random.fold_in(rng, 2), number_of)]


def deal_out(key, own, number, rows, amount, top, reach, skew):
    sequence = jax.random.permutation(key, amount)
    packed, ordinary = shares(amount, rows * top, reach, skew, True), shares(amount, rows * top, reach, skew, False)
    places = jnp.arange(amount)

    def named(sizes, offset_by):
        used = int((sizes > 0).sum())
        fixed = max(1, used // 4)
        shifted = fixed + (places - fixed + offset_by * (used - fixed)) % max(1, amount - fixed)
        return jnp.zeros((amount,), jnp.int32).at[sequence[jnp.where(places < fixed, places, shifted)]].set(jnp.asarray(sizes, jnp.int32))

    sizes = jnp.where(number % 4 == 0, named(packed, number // 4), named(ordinary, number - number // 4 - 1))
    mixed = jax.random.permutation(jax.random.fold_in(own, 3), amount)
    giver, receiver = mixed[0:amount // 2 * 2:2], mixed[1:amount // 2 * 2:2]
    margin = jnp.minimum(sizes[giver] - 1, reach - sizes[receiver]) // 2
    margin = jnp.where((giver == sequence[0]) | (receiver == sequence[0]) | (sizes[receiver] == 0), 0, jnp.maximum(margin, 0))
    shifted = jax.random.randint(jax.random.fold_in(own, 4), (amount // 2,), 0, 1 << 20) % (margin + 1)
    sizes = sizes.at[giver].add(-shifted).at[receiver].add(shifted)
    items = jnp.searchsorted(jnp.cumsum(sizes), jnp.arange(rows * top), side="right").astype(jnp.int32)
    grid = items.reshape(top, rows).T
    grid = grid[jax.random.permutation(jax.random.fold_in(own, 1), rows)]
    offset_by = jax.random.randint(jax.random.fold_in(own, 2), (rows, 1), 0, top)
    return jnp.take_along_axis(grid, (jnp.arange(top)[None, :] + offset_by) % top, axis=1)


def shares(amount, total, bound, slope, full):
    loads = [(1 << 20) // math.isqrt(grade ** slope) + 1 for grade in range(1, amount + 1)]
    largest = bound if full else min(bound, max(-(-total // amount), total * loads[0] // sum(loads)))
    least = 1 if total - largest >= amount - 1 else 0
    given, surplus = [largest] + [least] * (amount - 1), total - largest - least * (amount - 1)
    while surplus > 0:
        free = [i for i in range(1, amount) if given[i] < largest] or [i for i in range(1, amount) if given[i] < bound]
        pool, left = sum([loads[i] for i in free]), surplus
        for i in free:
            addition = min(bound - given[i], max(1, left * loads[i] // pool), surplus)
            given[i] = given[i] + addition
            surplus = surplus - addition
    return np.array(given)


def centred(rng, extent, spread, limit, shards=(), kind=jnp.bfloat16):
    gain = steps_of(rng, extent, shards, -0.22, 0.18) if shards else 1.0
    array = jax.random.normal(rng, extent, jnp.float32) * spread * gain
    return jnp.minimum(jnp.maximum(array, -limit), limit).astype(kind)


def gaussian_with(key, dims, scale, most, pieces, heavy, kind=jnp.bfloat16):
    result = scale * jax.random.normal(key, dims, jnp.float32)
    if pieces:
        result = result * steps_of(key, dims, pieces, -0.22, 0.18)
    return jnp.clip(strengthened(result, jax.random.fold_in(key, 3), *heavy), -most, most).astype(kind)


def setup_inputs(seed: int = 0) -> dict:
    keys = jax.random.split(jax.random.key(seed), 12)
    hidden_in = centred(keys[0], (TOKENS, D), 1.0, 6.0, ((0, 256),))
    w_query = centred(keys[1], (D, HEADS * HEAD_DIM), D ** -0.5, 0.09375, ((1, 64),))
    w_keyvalue = centred(keys[2], (D, KV_HEADS * 2 * HEAD_DIM), D ** -0.5, 0.09375, ((1, 64),))
    w_out = centred(keys[3], (HEADS * HEAD_DIM, D), HEAD_DIM ** -0.5, 0.5, ((0, 64),))
    key_gain = jnp.clip(1.0 + 0.18 * jax.random.normal(keys[4], (HEAD_DIM,), jnp.float32), 0.1, 1.9)
    router = centred(keys[5], (D, EXPERTS), (D * 8) ** -0.5, 0.03125)
    trainer_gate_up = gaussian_with(keys[6], (EXPERTS, D, 2, FFE), D ** -0.5, 0.25, ((1, 64), (3, 4)), (1, 0, 64, 4.0))
    trainer_down = gaussian_with(keys[7], (EXPERTS, FFE, D), (FFE // 9) ** -0.5, 1.5, ((1, 64), (2, 4)), (1, 0, 64, 4.0))
    expert_ids_keys = jax.random.split(jax.random.fold_in(keys[8], 1), TOKENS // TOK_DEV)
    expert_ids_turns = jax.random.permutation(jax.random.fold_in(keys[8], 3), TOKENS // TOK_DEV)
    expert_ids = jax.vmap(lambda own, number: deal_out(jax.random.fold_in(keys[8], 2), own, number, TOK_DEV, EXPERTS, TOP, CAP, 2))(expert_ids_keys, expert_ids_turns).reshape((TOKENS, TOP))
    seq_lengths = ragged(keys[9], NSEQ, TOKENS, TOKENS * 3 // 4, 1).astype(jnp.int32)
    seq_offsets = jax.random.randint(keys[10], (NSEQ,), 0, 4097).astype(jnp.int32)
    return {"hidden_in": hidden_in, "w_query": w_query, "w_keyvalue": w_keyvalue, "w_out": w_out, "key_gain": key_gain, "router": router, "trainer_gate_up": trainer_gate_up, "trainer_down": trainer_down, "expert_ids": expert_ids, "seq_lengths": seq_lengths, "seq_offsets": seq_offsets}


EPSILON = 1e-06
THETA = 1000000.0

def rms_rows(values):
    return values * lax.rsqrt(lax.optimization_barrier(jnp.mean(values * values, axis=-1, keepdims=True)) + EPSILON)

def rotate(values, angles):
    half = values.shape[-1] // 2
    cosine = jnp.cos(angles)
    sine = jnp.sin(angles)
    first = values[..., :half]
    second = values[..., half:]
    return jnp.concatenate([first * cosine - second * sine, second * cosine + first * sine], axis=-1)

def layout(seq_lengths, seq_offsets, places):
    bounds = jnp.cumsum(seq_lengths)
    starts = bounds - seq_lengths
    segment = lax.optimization_barrier(jnp.sum((places[:, None] >= bounds[None, :-1]).astype(jnp.int32), axis=1))
    member = segment[:, None] == jnp.arange(seq_lengths.shape[0], dtype=jnp.int32)[None, :]
    begin = lax.optimization_barrier(jnp.sum(jnp.where(member, starts[None, :], 0), axis=1))
    offset = lax.optimization_barrier(jnp.sum(jnp.where(member, seq_offsets[None, :], 0), axis=1))
    return (segment, offset + places - begin)

def angles_for(position, head_dim):
    inverse = THETA ** (-(jnp.arange(head_dim // 2, dtype=jnp.float32) * 2.0 / head_dim))
    return position.astype(jnp.float32)[:, None] * inverse[None, :]

def rounded(values):
    return lax.optimization_barrier(values.astype(jnp.bfloat16))

def reference(hidden_in, w_query, w_keyvalue, w_out, key_gain, router, trainer_gate_up, trainer_down, expert_ids, seq_lengths, seq_offsets):
    hidden = hidden_in.astype(jnp.float32)
    normed_in = rms_rows(hidden).astype(jnp.bfloat16)
    places = jnp.arange(TOKENS, dtype=jnp.int32)
    segment, position = layout(seq_lengths, seq_offsets, places)
    angles = angles_for(position, HEAD_DIM)
    kv_raw = rounded(jnp.dot(normed_in, w_keyvalue, preferred_element_type=jnp.float32))
    kv_raw = kv_raw.reshape(TOKENS, 2, HEAD_DIM, KV_HEADS)
    key_source = kv_raw[:, 0].transpose(0, 2, 1).astype(jnp.float32)
    key_rows = rotate(rms_rows(key_source) * key_gain, angles[:, None, :]).astype(jnp.bfloat16)
    value_rows = kv_raw[:, 1].transpose(0, 2, 1)
    kv_cache = jnp.stack([key_rows, value_rows], axis=1).transpose(1, 3, 2, 0).reshape(2 * HEAD_DIM * KV_HEADS, TOKENS)
    query_full = jnp.dot(normed_in, w_query, preferred_element_type=jnp.float32).reshape(TOKENS, HEADS, HEAD_DIM)
    queries = rotate(rms_rows(query_full), angles[:, None, :]).astype(jnp.bfloat16)
    allowed = (segment[:, None] == segment[None, :]) & (places[None, :] <= places[:, None])
    group = HEADS // KV_HEADS
    scale = 1.0 / math.sqrt(HEAD_DIM)

    def one_head(head):
        query_one = lax.dynamic_index_in_dim(queries, head, 1, keepdims=False).astype(jnp.float32)
        key_one = lax.dynamic_index_in_dim(key_rows, head // group, 1, keepdims=False).astype(jnp.float32)
        value_one = lax.dynamic_index_in_dim(value_rows, head // group, 1, keepdims=False).astype(jnp.float32)
        scores = jnp.dot(query_one, key_one.T, precision=lax.Precision.HIGHEST) * scale
        weights = jnp.where(allowed, jnp.exp(scores), 0.0)
        numerator = jnp.dot(rounded(weights).astype(jnp.float32), value_one, precision=lax.Precision.HIGHEST)
        return (numerator / lax.optimization_barrier(jnp.sum(weights, axis=1))[:, None]).astype(jnp.bfloat16)
    context = lax.map(one_head, jnp.arange(HEADS, dtype=jnp.int32))
    context = context.transpose(1, 0, 2).reshape(TOKENS, HEADS * HEAD_DIM)
    resid = rounded(hidden + jnp.dot(context, w_out, preferred_element_type=jnp.float32)).astype(jnp.float32)
    normed = rms_rows(resid).astype(jnp.bfloat16)
    logits = jnp.dot(normed, router, preferred_element_type=jnp.float32)
    chosen = jnp.take_along_axis(logits, expert_ids, axis=1)
    gates = jax.nn.softmax(chosen, axis=1)
    most = N_SEQ * N_EXPERT * CAP

    def one_expert(total, expert):
        hit = expert_ids == expert
        weight = lax.optimization_barrier(jnp.sum(jnp.where(hit, gates, 0.0), axis=1))
        used = jnp.any(hit, axis=1)
        count = jnp.sum(used.astype(jnp.int32))
        index = jnp.nonzero(used, size=most, fill_value=0)[0]
        valid = jnp.arange(most) < count
        rows = normed[index]
        both = jnp.dot(rows, trainer_gate_up[expert].reshape(D, 2 * FFE), preferred_element_type=jnp.float32)
        both = both.reshape(most, 2, FFE)
        act = (jax.nn.silu(both[:, 0]) * both[:, 1]).astype(jnp.bfloat16)
        out_rows = rounded(jnp.dot(act, trainer_down[expert], preferred_element_type=jnp.float32)).astype(jnp.float32)
        row_weight = jnp.where(valid, weight[index], 0.0)
        return (total.at[index].add(row_weight[:, None] * out_rows), 0)
    moe, unused = lax.scan(one_expert, jnp.zeros((TOKENS, D), jnp.float32), jnp.arange(EXPERTS, dtype=jnp.int32))
    mixed = (resid + moe).astype(jnp.bfloat16)
    return (mixed, kv_cache)
```

```python
import math

import jax
import jax.numpy as jnp
from jax import lax
from jax.sharding import Mesh, PartitionSpec as P

HEADS = 64
KV_HEADS = 4
CAP = 2
EPSILON = 1e-06
THETA = 1000000.0

PLANE = ("y", "core")
EXPERT = ("z", "y", "core")
BF = jnp.bfloat16
F32 = jnp.float32


def rms_rows(values):
    return values * lax.rsqrt(jnp.mean(values * values, axis=-1, keepdims=True) + EPSILON)


def rotate(values, cosine, sine):
    half = values.shape[-1] // 2
    first = values[..., :half]
    second = values[..., half:]
    return jnp.concatenate(
        [first * cosine - second * sine, second * cosine + first * sine], axis=-1
    )


def layout(seq_lengths, seq_offsets, places):
    bounds = jnp.cumsum(seq_lengths)
    starts = bounds - seq_lengths
    segment = jnp.sum((places[:, None] >= bounds[None, :-1]).astype(jnp.int32), axis=1)
    member = segment[:, None] == jnp.arange(seq_lengths.shape[0], dtype=jnp.int32)[None, :]
    begin = jnp.sum(jnp.where(member, starts[None, :], 0), axis=1)
    offset = jnp.sum(jnp.where(member, seq_offsets[None, :], 0), axis=1)
    return (segment, offset + places - begin)


def angles_for(position, head_dim):
    inverse = THETA ** (-(jnp.arange(head_dim // 2, dtype=F32) * 2.0 / head_dim))
    return position.astype(F32)[:, None] * inverse[None, :]


def exchange(value, axes):
    return lax.all_to_all(value, axes, split_axis=0, concat_axis=0, tiled=True)


def swap(value, axis, mask):
    size = lax.axis_size(axis)
    return lax.ppermute(value, axis, [(i, i ^ mask) for i in range(size)])


def around(value, axis):
    return [value] + [swap(value, axis, k) for k in range(1, lax.axis_size(axis))]


def turn(blocks, place):
    blocks, bit = list(blocks), 1
    while bit < len(blocks):
        flip = (place & bit) != 0
        blocks = [jnp.where(flip, blocks[i ^ bit], blocks[i]) for i in range(len(blocks))]
        bit = bit * 2
    return blocks


def trade(blocks, axis, place):
    mine = turn(blocks, place)
    return [mine[0]] + [swap(mine[k], axis, k) for k in range(1, len(mine))]


def total(blocks):
    return sum(block.astype(F32) for block in blocks[1:]) + blocks[0].astype(F32)


def shards(
    hidden_in,
    w_query,
    w_keyvalue,
    w_out,
    key_gain,
    router,
    trainer_gate_up,
    trainer_down,
    expert_ids,
    seq_lengths,
    seq_offsets,
):
    n_seq = lax.axis_size("seq")
    n_z = lax.axis_size("z")
    n_y = lax.axis_size("y")
    n_core = lax.axis_size("core")
    n_plane = n_y * n_core
    n_owner = n_z * n_plane
    x_at = lax.axis_index("seq")
    z_at = lax.axis_index("z")
    y_at = lax.axis_index("y")
    c_at = lax.axis_index("core")
    p_at = y_at * n_core + c_at
    tok_own, width = hidden_in.shape
    head_dim = key_gain.shape[0]
    piece = width // n_plane
    tok_part = tok_own * n_plane
    tok_shard = tok_part * n_z
    kv_dims = w_keyvalue.shape[1] // KV_HEADS
    top_count = expert_ids.shape[1]
    n_experts = router.shape[1]

    with jax.named_scope("weights"):
        query_w = exchange(w_query.reshape(n_plane, piece, head_dim), PLANE)
        kv_w = w_keyvalue.T.reshape(kv_dims, KV_HEADS, n_plane, piece).transpose(1, 2, 0, 3)
        kv_w = jnp.broadcast_to(kv_w[:, None], (KV_HEADS, n_z // KV_HEADS) + kv_w.shape[1:])
        kv_w = exchange(kv_w.reshape(n_owner, kv_dims, piece), EXPERT)
        kv_w = kv_w.reshape(n_owner * kv_dims, piece)
        out_w = w_out.reshape(head_dim, n_y, n_core, piece).transpose(2, 1, 0, 3)
        out_w = turn(trade([out_w[0], out_w[1]], "core", c_at), c_at)
        out_w = jnp.stack(out_w, axis=1)
        out_w = turn(trade([out_w[i] for i in range(n_y)], "y", y_at), y_at)
        out_w = jnp.concatenate(out_w, axis=0).reshape(n_plane * head_dim, piece)

    gate_up_served = exchange(trainer_gate_up, EXPERT)
    gate_up = gate_up_served.reshape(width, 2, -1)

    with jax.named_scope("tokens"):
        hidden = hidden_in.astype(F32)
        normed_own = rms_rows(hidden).astype(BF)
        cut = normed_own.reshape(tok_own, n_y, n_core, piece).transpose(2, 1, 0, 3)
        cut = jnp.stack(turn(trade([cut[0], cut[1]], "core", c_at), c_at), axis=1)
        cut = turn(trade([cut[i] for i in range(n_y)], "y", y_at), y_at)
        cut = jnp.stack(cut).reshape(tok_part, piece)
        pieces = jnp.concatenate(around(cut, "z"), axis=0)

    with jax.named_scope("projections"):
        query_part = jnp.einsum("tp,hpd->thd", pieces, query_w, preferred_element_type=F32)
        kv_part = lax.dot_general(
            pieces, kv_w, (((1,), (1,)), ((), ())), preferred_element_type=F32
        )
        parts = jnp.concatenate([query_part.reshape(tok_shard, -1), kv_part], axis=1).astype(BF)
        parts = parts.reshape(n_y, n_core, tok_part, -1)
        parts = total(trade([parts[:, 0], parts[:, 1]], "core", c_at)).astype(BF)
        sums = total(trade([parts[i] for i in range(n_y)], "y", y_at))
        query_full = sums[:, : n_plane * head_dim].reshape(tok_part, n_plane, head_dim)
        kv_mine = sums[:, n_plane * head_dim :].astype(BF)

    block = z_at ^ p_at
    inside = jnp.arange(tok_part, dtype=jnp.int32)
    places = x_at * tok_shard + block * tok_part + inside
    segment, position = layout(seq_lengths, seq_offsets, places)
    angles = angles_for(position, head_dim)
    cosine, sine = jnp.cos(angles), jnp.sin(angles)

    with jax.named_scope("keys"):
        key_mine = rms_rows(kv_mine[:, :head_dim].astype(F32)) * key_gain
        key_mine = rotate(key_mine, cosine, sine).astype(BF)
        kv_mine = jnp.concatenate([key_mine, kv_mine[:, head_dim:]], axis=1)
        near = jnp.stack(around(kv_mine, "seq"))
        near = jnp.stack(around(near, "y"))
        near = jnp.stack(around(near, "core"))
        near = near.reshape(n_core * n_y * n_seq * tok_part, 2 * head_dim)
        keys, values = near[:, :head_dim], near[:, head_dim:]
        rel = jnp.arange(n_plane * n_seq, dtype=jnp.int32)
        rel_c, rel_y, rel_x = rel // (n_y * n_seq), rel // n_seq % n_y, rel % n_seq
        begins = (x_at ^ rel_x) * tok_shard + (block ^ (rel_y * n_core + rel_c)) * tok_part
        key_places = (begins[:, None] + inside[None, :]).reshape(-1)

    with jax.named_scope("attention"):
        queries = rotate(rms_rows(query_full), cosine[:, None], sine[:, None]).astype(BF)
        key_segments, unused = layout(seq_lengths, seq_offsets, key_places)
        scores = jnp.einsum("qhd,kd->qhk", queries, keys, preferred_element_type=F32)
        allowed = (segment[:, None] == key_segments[None, :]) & (
            key_places[None, :] <= places[:, None]
        )
        weights = jnp.where(
            allowed[:, None, :], jnp.exp(scores * (1.0 / math.sqrt(head_dim))), 0.0
        )
        numerator = jnp.einsum(
            "qhk,kd->qhd", weights.astype(BF), values, preferred_element_type=F32
        )
        context = (numerator / jnp.sum(weights, axis=2)[..., None]).astype(BF)

    with jax.named_scope("output"):
        context = context.reshape(tok_part, n_plane * head_dim)
        context = jnp.stack(around(context, "y"))
        context = jnp.stack(around(context, "core"))
        context = context.reshape(tok_shard, n_plane * head_dim)
        out_part = jnp.dot(context, out_w, preferred_element_type=F32).astype(BF)
        out_part = out_part.reshape(n_core, n_y, tok_part, piece)
        out_part = jnp.stack(turn([out_part[0], out_part[1]], c_at), axis=1)
        out_part = turn([out_part[i] for i in range(n_y)], y_at)
        out_part = jnp.stack(out_part).reshape(n_plane, tok_part, piece)
        shares = [out_part[0]] + [swap(out_part[k], "z", k) for k in range(1, n_z)]
        own = total(shares).astype(BF).reshape(n_y, n_core, tok_own, piece)
        own = jnp.stack(turn(trade([own[:, 0], own[:, 1]], "core", c_at), c_at), axis=1)
        own = turn(trade([own[i] for i in range(n_y)], "y", y_at), y_at)
        own = jnp.stack(own).reshape(n_plane, tok_own, piece).transpose(1, 0, 2)
        resid = (hidden + own.reshape(tok_own, width).astype(F32)).astype(BF)
        resid_wide = resid.astype(F32)
        normed = rms_rows(resid_wide).astype(BF)

    normed, gate_up, kv_mine = lax.optimization_barrier((normed, gate_up, kv_mine))

    with jax.named_scope("cache"):
        cache = kv_mine.T.reshape(n_owner, kv_dims, tok_part)
        cache = exchange(cache, EXPERT).reshape(n_z, n_plane, kv_dims, tok_part)
        step = n_z // KV_HEADS
        cache = jnp.stack(
            [
                jnp.stack([cache[step * k, t ^ (step * k)] for t in range(n_plane)], axis=1)
                for k in range(KV_HEADS)
            ],
            axis=1,
        )
        kv_cache = cache.reshape(kv_dims * KV_HEADS, tok_shard)

    def placing_of(ids):
        picked = ids[:, :, None] == jnp.arange(n_experts, dtype=jnp.int32)[None, None, :]
        used = jnp.any(picked, axis=1)
        earlier = jnp.cumsum(used.astype(jnp.int32), axis=0) - used.astype(jnp.int32)
        return picked, used[:, :, None] & (
            earlier[:, :, None] == jnp.arange(CAP, dtype=jnp.int32)[None, None, :]
        )

    with jax.named_scope("dispatch"):
        picked, placing = placing_of(expert_ids)
        dispatch_matrix = placing.reshape(tok_own, n_experts * CAP).T.astype(BF)
        send_buffer = jnp.dot(dispatch_matrix, normed, preferred_element_type=F32).astype(BF)
        arrived = exchange(send_buffer.reshape(n_experts, CAP, width), EXPERT)
        arrived = arrived.reshape(n_owner * CAP, width)
        half = arrived.shape[0] // 2
        near_rows, far_rows = swap(arrived, "seq", 1), swap(arrived, "seq", 3)
        top_rows, low_rows = swap(far_rows[:half], "seq", 1), swap(near_rows[half:], "seq", 3)
        expert_rows = [arrived, near_rows, jnp.concatenate([top_rows, low_rows], axis=0), far_rows]
        logits = jnp.dot(normed, router, preferred_element_type=F32)
        chosen = jnp.sum(jnp.where(picked, logits[:, None, :], 0.0), axis=2)
        gates = jax.nn.softmax(chosen, axis=1)

    with jax.named_scope("experts"):
        down_served = exchange(trainer_down, EXPERT)
        down = down_served.reshape(n_seq, -1, trainer_down.shape[2])
        down = turn([down[i] for i in range(n_seq)], x_at)

        def act_of(rows):
            both = jnp.einsum("rd,dgf->grf", rows, gate_up, preferred_element_type=F32)
            return (jax.nn.silu(both[0]) * both[1]).astype(BF)

        act = jnp.concatenate([act_of(rows) for rows in expert_rows], axis=0)
        gates_high = gates.astype(BF)
        gates_low = (gates - gates_high.astype(F32)).astype(BF)
        gate_block = jnp.concatenate([gates_high, gates_low], axis=0)
        ids_block = jnp.concatenate([expert_ids, expert_ids], axis=0).astype(BF)
        gate_pad = jnp.zeros((2 * tok_own, act.shape[1] - 2 * top_count), BF)
        gate_block = jnp.concatenate([gate_block, ids_block, gate_pad], axis=1)
        n_rows = act.shape[0]
        wide = around(jnp.concatenate([act, gate_block], axis=0), "seq")
        blocks = [piece_of[n_rows:].astype(F32) for piece_of in wide]
        gates_all = jnp.stack([b[:tok_own, :top_count] + b[tok_own:, :top_count] for b in blocks])
        ids_all = jnp.stack([b[:tok_own, top_count : 2 * top_count] for b in blocks])
        ids_all = ids_all.astype(jnp.int32)
        shape = (n_seq, n_rows // n_seq, -1)
        outputs = 0.0
        for k in range(n_seq):
            from_k = wide[k][:n_rows].reshape(shape)
            from_k = jnp.concatenate([from_k[j ^ k] for j in range(n_seq)], axis=0)
            outputs = outputs + jnp.dot(from_k, down[k], preferred_element_type=F32)
        outputs = outputs.astype(BF)

    with jax.named_scope("combine"):
        columns = outputs.shape[1]
        outputs = outputs.reshape(n_seq, n_owner, CAP, columns).transpose(1, 0, 2, 3)
        returned = exchange(outputs.reshape(n_owner, n_seq * CAP, columns), EXPERT)
        returned = returned.reshape(n_owner, n_seq, CAP, columns)
        picked_all, placing_all = jax.vmap(placing_of)(ids_all)
        gate_of = jnp.sum(jnp.where(picked_all, gates_all[:, :, :, None], 0.0), axis=2)
        combine_matrix = jnp.where(placing_all, gate_of[:, :, :, None], 0.0)
        combine_high = combine_matrix.astype(BF)
        combine_low = (combine_matrix - combine_high.astype(F32)).astype(BF)
        rows = returned.transpose(1, 0, 2, 3).reshape(n_seq, n_owner * CAP, columns)
        combine_both = jnp.concatenate([combine_high, combine_low], axis=1)
        moe = jnp.einsum(
            "xts,xsc->xtc",
            combine_both.reshape(n_seq, 2 * tok_own, n_experts * CAP),
            rows,
            preferred_element_type=F32,
        )
        moe = (moe[:, :tok_own] + moe[:, tok_own:]).astype(BF)
        moe = [moe[0]] + [swap(moe[k], "seq", k) for k in range(1, n_seq)]
        moe = jnp.concatenate(turn(moe, x_at), axis=1)
        mixed = (resid_wide + moe.astype(F32)).astype(BF)
    return (mixed, kv_cache)


def solution(mesh):
    n_seq, n_owner = mesh.devices.shape
    grid = Mesh(mesh.devices.reshape(n_seq, n_owner // 8, 4, 2), ("seq", "z", "y", "core"))
    in_specs = (
        P(("seq",) + EXPERT, None),
        P(None, EXPERT),
        P(None, EXPERT),
        P(EXPERT, None),
        P(),
        P(),
        P(None, EXPERT, None, "seq"),
        P(None, EXPERT, "seq"),
        P(("seq",) + EXPERT, None),
        P(),
        P(),
    )
    out_specs = (P(("seq",) + EXPERT, None), P(EXPERT, "seq"))
    return jax.shard_map(shards, mesh=grid, in_specs=in_specs, out_specs=out_specs, check_vma=False)
```

```python
import math

import jax
import jax.numpy as jnp
from jax import lax
from jax.sharding import Mesh, PartitionSpec as P

HEADS = 64
KV_HEADS = 4
CAP = 2
EPSILON = 1e-06
THETA = 1000000.0

PLANE = ("y", "core")
EXPERT = ("z", "y", "core")
BF = jnp.bfloat16
F32 = jnp.float32


def rms_rows(values):
    return values * lax.rsqrt(jnp.mean(values * values, axis=-1, keepdims=True) + EPSILON)


def rotate(values, cosine, sine):
    half = values.shape[-1] // 2
    first = values[..., :half]
    second = values[..., half:]
    return jnp.concatenate(
        [first * cosine - second * sine, second * cosine + first * sine], axis=-1
    )


def layout(seq_lengths, seq_offsets, places):
    bounds = jnp.cumsum(seq_lengths)
    starts = bounds - seq_lengths
    segment = jnp.sum((places[:, None] >= bounds[None, :-1]).astype(jnp.int32), axis=1)
    member = segment[:, None] == jnp.arange(seq_lengths.shape[0], dtype=jnp.int32)[None, :]
    begin = jnp.sum(jnp.where(member, starts[None, :], 0), axis=1)
    offset = jnp.sum(jnp.where(member, seq_offsets[None, :], 0), axis=1)
    return (segment, offset + places - begin)


def angles_for(position, head_dim):
    inverse = THETA ** (-(jnp.arange(head_dim // 2, dtype=F32) * 2.0 / head_dim))
    return position.astype(F32)[:, None] * inverse[None, :]


def exchange(value, axes):
    return lax.all_to_all(value, axes, split_axis=0, concat_axis=0, tiled=True)


def swap(value, axis, mask):
    size = lax.axis_size(axis)
    return lax.ppermute(value, axis, [(i, i ^ mask) for i in range(size)])


def around(value, axis):
    return [value] + [swap(value, axis, k) for k in range(1, lax.axis_size(axis))]


def turn(blocks, place):
    blocks, bit = list(blocks), 1
    while bit < len(blocks):
        flip = (place & bit) != 0
        blocks = [jnp.where(flip, blocks[i ^ bit], blocks[i]) for i in range(len(blocks))]
        bit = bit * 2
    return blocks


def trade(blocks, axis, place):
    mine = turn(blocks, place)
    return [mine[0]] + [swap(mine[k], axis, k) for k in range(1, len(mine))]


def total(blocks):
    return sum(block.astype(F32) for block in blocks[1:]) + blocks[0].astype(F32)


def shards(
    hidden_in,
    w_query,
    w_keyvalue,
    w_out,
    key_gain,
    router,
    trainer_gate_up,
    trainer_down,
    expert_ids,
    seq_lengths,
    seq_offsets,
):
    n_seq = lax.axis_size("seq")
    n_z = lax.axis_size("z")
    n_y = lax.axis_size("y")
    n_core = lax.axis_size("core")
    n_plane = n_y * n_core
    n_owner = n_z * n_plane
    x_at = lax.axis_index("seq")
    z_at = lax.axis_index("z")
    y_at = lax.axis_index("y")
    c_at = lax.axis_index("core")
    p_at = y_at * n_core + c_at
    tok_own, width = hidden_in.shape
    head_dim = key_gain.shape[0]
    piece = width // n_plane
    tok_part = tok_own * n_plane
    tok_shard = tok_part * n_z
    kv_dims = w_keyvalue.shape[1] // KV_HEADS
    top_count = expert_ids.shape[1]
    n_experts = router.shape[1]

    with jax.named_scope("tokens"):
        hidden = hidden_in.astype(F32)
        normed_own = rms_rows(hidden).astype(BF)
        cut = normed_own.reshape(tok_own, n_y, n_core, piece).transpose(2, 1, 0, 3)
        cut = jnp.stack(turn(trade([cut[0], cut[1]], "core", c_at), c_at), axis=1)
        cut = turn(trade([cut[i] for i in range(n_y)], "y", y_at), y_at)
        cut = jnp.stack(cut).reshape(tok_part, piece)
    with jax.named_scope("weights"):
        cut, w_query, w_keyvalue = lax.optimization_barrier((cut, w_query, w_keyvalue))
        query_w = exchange(w_query.reshape(n_plane, piece, head_dim), PLANE)
        kv_w = w_keyvalue.T.reshape(kv_dims, KV_HEADS, n_plane, piece).transpose(1, 2, 0, 3)
        kv_w = jnp.broadcast_to(kv_w[:, None], (KV_HEADS, n_z // KV_HEADS) + kv_w.shape[1:])
        kv_w = exchange(kv_w.reshape(n_owner, kv_dims, piece), EXPERT)
        kv_w = kv_w.reshape(n_owner * kv_dims, piece)
        out_w = w_out.reshape(head_dim, n_y, n_core, piece).transpose(2, 1, 0, 3)
        out_w = turn(trade([out_w[0], out_w[1]], "core", c_at), c_at)
        out_w = jnp.stack(out_w, axis=1)
        out_w = turn(trade([out_w[i] for i in range(n_y)], "y", y_at), y_at)
        out_w = jnp.concatenate(out_w, axis=0).reshape(n_plane * head_dim, piece)

    gate_up_served = exchange(trainer_gate_up, EXPERT)
    gate_up = gate_up_served.reshape(width, 2, -1)

    with jax.named_scope("spread"):
        pieces = jnp.concatenate(around(cut, "z"), axis=0)
        pieces, out_w = lax.optimization_barrier((pieces, out_w))

    with jax.named_scope("projections"):
        query_part = jnp.einsum("tp,hpd->thd", pieces, query_w, preferred_element_type=F32)
        kv_part = lax.dot_general(
            pieces, kv_w, (((1,), (1,)), ((), ())), preferred_element_type=F32
        )
        parts = jnp.concatenate([query_part.reshape(tok_shard, -1), kv_part], axis=1).astype(BF)
        parts = parts.reshape(n_y, n_core, tok_part, -1)
        parts = total(trade([parts[:, 0], parts[:, 1]], "core", c_at)).astype(BF)
        sums = total(trade([parts[i] for i in range(n_y)], "y", y_at))
        query_full = sums[:, : n_plane * head_dim].reshape(tok_part, n_plane, head_dim)
        kv_mine = sums[:, n_plane * head_dim :].astype(BF)

    block = z_at ^ p_at
    inside = jnp.arange(tok_part, dtype=jnp.int32)
    places = x_at * tok_shard + block * tok_part + inside
    segment, position = layout(seq_lengths, seq_offsets, places)
    angles = angles_for(position, head_dim)
    cosine, sine = jnp.cos(angles), jnp.sin(angles)

    with jax.named_scope("keys"):
        key_mine = rms_rows(kv_mine[:, :head_dim].astype(F32)) * key_gain
        key_mine = rotate(key_mine, cosine, sine).astype(BF)
        kv_mine = jnp.concatenate([key_mine, kv_mine[:, head_dim:]], axis=1)
        near = jnp.stack(around(kv_mine, "seq"))
        near = jnp.stack(around(near, "y"))
        near = jnp.stack(around(near, "core"))
        near = near.reshape(n_core * n_y * n_seq * tok_part, 2 * head_dim)
        keys, values = near[:, :head_dim], near[:, head_dim:]
        rel = jnp.arange(n_plane * n_seq, dtype=jnp.int32)
        rel_c, rel_y, rel_x = rel // (n_y * n_seq), rel // n_seq % n_y, rel % n_seq
        begins = (x_at ^ rel_x) * tok_shard + (block ^ (rel_y * n_core + rel_c)) * tok_part
        key_places = (begins[:, None] + inside[None, :]).reshape(-1)

    with jax.named_scope("attention"):
        queries = rotate(rms_rows(query_full), cosine[:, None], sine[:, None]).astype(BF)
        key_segments, unused = layout(seq_lengths, seq_offsets, key_places)
        scores = jnp.einsum("qhd,kd->qhk", queries, keys, preferred_element_type=F32)
        allowed = (segment[:, None] == key_segments[None, :]) & (
            key_places[None, :] <= places[:, None]
        )
        weights = jnp.where(
            allowed[:, None, :], jnp.exp(scores * (1.0 / math.sqrt(head_dim))), 0.0
        )
        numerator = jnp.einsum(
            "qhk,kd->qhd", weights.astype(BF), values, preferred_element_type=F32
        )
        context = (numerator / jnp.sum(weights, axis=2)[..., None]).astype(BF)

    with jax.named_scope("output"):
        context = context.reshape(tok_part, n_plane * head_dim)
        context = jnp.stack(around(context, "y"))
        context = jnp.stack(around(context, "core"))
        context = context.reshape(tok_shard, n_plane * head_dim)
        out_part = jnp.dot(context, out_w, preferred_element_type=F32).astype(BF)
        out_part = out_part.reshape(n_core, n_y, tok_part, piece)
        out_part = jnp.stack(turn([out_part[0], out_part[1]], c_at), axis=1)
        out_part = turn([out_part[i] for i in range(n_y)], y_at)
        out_part = jnp.stack(out_part).reshape(n_plane, tok_part, piece)
        shares = [out_part[0]] + [swap(out_part[k], "z", k) for k in range(1, n_z)]
        own = total(shares).astype(BF).reshape(n_y, n_core, tok_own, piece)
        own = jnp.stack(turn(trade([own[:, 0], own[:, 1]], "core", c_at), c_at), axis=1)
        own = turn(trade([own[i] for i in range(n_y)], "y", y_at), y_at)
        own = jnp.stack(own).reshape(n_plane, tok_own, piece).transpose(1, 0, 2)
        resid = (hidden + own.reshape(tok_own, width).astype(F32)).astype(BF)
        resid_wide = resid.astype(F32)
        normed = rms_rows(resid_wide).astype(BF)

    normed, gate_up = lax.optimization_barrier((normed, gate_up))

    def placing_of(ids):
        picked = ids[:, :, None] == jnp.arange(n_experts, dtype=jnp.int32)[None, None, :]
        used = jnp.any(picked, axis=1)
        earlier = jnp.cumsum(used.astype(jnp.int32), axis=0) - used.astype(jnp.int32)
        return picked, used[:, :, None] & (
            earlier[:, :, None] == jnp.arange(CAP, dtype=jnp.int32)[None, None, :]
        )

    with jax.named_scope("dispatch"):
        picked, placing = placing_of(expert_ids)
        dispatch_matrix = placing.reshape(tok_own, n_experts * CAP).T.astype(BF)
        send_buffer = jnp.dot(dispatch_matrix, normed, preferred_element_type=F32).astype(BF)
        cache = kv_mine.T.reshape(n_owner, CAP, kv_dims * tok_part // CAP)
        send_buffer = send_buffer.reshape(n_experts, CAP, width)
        arrived = exchange(jnp.concatenate([send_buffer, cache], axis=2), EXPERT)
        cache = arrived[:, :, width:].reshape(n_z, n_plane, kv_dims, tok_part)
        arrived = arrived[:, :, :width].reshape(n_owner * CAP, width)
        arrived, trainer_down = lax.optimization_barrier((arrived, trainer_down))
        step = n_z // KV_HEADS
        cache = jnp.stack(
            [
                jnp.stack([cache[step * k, t ^ (step * k)] for t in range(n_plane)], axis=1)
                for k in range(KV_HEADS)
            ],
            axis=1,
        )
        kv_cache = cache.reshape(kv_dims * KV_HEADS, tok_shard)
        half = arrived.shape[0] // 2
        near_rows, far_rows = swap(arrived, "seq", 1), swap(arrived, "seq", 3)
        top_rows, low_rows = swap(far_rows[:half], "seq", 1), swap(near_rows[half:], "seq", 3)
        expert_rows = [arrived, near_rows, jnp.concatenate([top_rows, low_rows], axis=0), far_rows]
        logits = jnp.dot(normed, router, preferred_element_type=F32)
        chosen = jnp.sum(jnp.where(picked, logits[:, None, :], 0.0), axis=2)
        gates = jax.nn.softmax(chosen, axis=1)

    with jax.named_scope("experts"):
        down_served = exchange(trainer_down, EXPERT)
        down = down_served.reshape(n_seq, -1, trainer_down.shape[2])
        down = turn([down[i] for i in range(n_seq)], x_at)

        def act_of(rows):
            both = jnp.einsum("rd,dgf->grf", rows, gate_up, preferred_element_type=F32)
            return (jax.nn.silu(both[0]) * both[1]).astype(BF)

        act = jnp.concatenate([act_of(rows) for rows in expert_rows], axis=0)
        gates_high = gates.astype(BF)
        gates_low = (gates - gates_high.astype(F32)).astype(BF)
        gate_block = jnp.concatenate([gates_high, gates_low], axis=0)
        ids_block = jnp.concatenate([expert_ids, expert_ids], axis=0).astype(BF)
        gate_pad = jnp.zeros((2 * tok_own, act.shape[1] - 2 * top_count), BF)
        gate_block = jnp.concatenate([gate_block, ids_block, gate_pad], axis=1)
        n_rows = act.shape[0]
        wide = around(jnp.concatenate([act, gate_block], axis=0), "seq")
        blocks = [piece_of[n_rows:].astype(F32) for piece_of in wide]
        gates_all = jnp.stack([b[:tok_own, :top_count] + b[tok_own:, :top_count] for b in blocks])
        ids_all = jnp.stack([b[:tok_own, top_count : 2 * top_count] for b in blocks])
        ids_all = ids_all.astype(jnp.int32)
        shape = (n_seq, n_rows // n_seq, -1)
        outputs = 0.0
        for k in range(n_seq):
            from_k = wide[k][:n_rows].reshape(shape)
            from_k = jnp.concatenate([from_k[j ^ k] for j in range(n_seq)], axis=0)
            outputs = outputs + jnp.dot(from_k, down[k], preferred_element_type=F32)
        outputs = outputs.astype(BF)

    with jax.named_scope("combine"):
        columns = outputs.shape[1]
        outputs = outputs.reshape(n_seq, n_owner, CAP, columns).transpose(1, 0, 2, 3)
        returned = exchange(outputs.reshape(n_owner, n_seq * CAP, columns), EXPERT)
        returned = returned.reshape(n_owner, n_seq, CAP, columns)
        picked_all, placing_all = jax.vmap(placing_of)(ids_all)
        gate_of = jnp.sum(jnp.where(picked_all, gates_all[:, :, :, None], 0.0), axis=2)
        combine_matrix = jnp.where(placing_all, gate_of[:, :, :, None], 0.0)
        combine_high = combine_matrix.astype(BF)
        combine_low = (combine_matrix - combine_high.astype(F32)).astype(BF)
        rows = returned.transpose(1, 0, 2, 3).reshape(n_seq, n_owner * CAP, columns)
        combine_both = jnp.concatenate([combine_high, combine_low], axis=1)
        moe = jnp.einsum(
            "xts,xsc->xtc",
            combine_both.reshape(n_seq, 2 * tok_own, n_experts * CAP),
            rows,
            preferred_element_type=F32,
        )
        moe = (moe[:, :tok_own] + moe[:, tok_own:]).astype(BF)
        moe = [moe[0]] + [swap(moe[k], "seq", k) for k in range(1, n_seq)]
        moe = jnp.concatenate(turn(moe, x_at), axis=1)
        mixed = (resid_wide + moe.astype(F32)).astype(BF)
    return (mixed, kv_cache)


def solution(mesh):
    n_seq, n_owner = mesh.devices.shape
    grid = Mesh(mesh.devices.reshape(n_seq, n_owner // 8, 4, 2), ("seq", "z", "y", "core"))
    in_specs = (
        P(("seq",) + EXPERT, None),
        P(None, EXPERT),
        P(None, EXPERT),
        P(EXPERT, None),
        P(),
        P(),
        P(None, EXPERT, None, "seq"),
        P(None, EXPERT, "seq"),
        P(("seq",) + EXPERT, None),
        P(),
        P(),
    )
    out_specs = (P(("seq",) + EXPERT, None), P(EXPERT, "seq"))
    return jax.shard_map(shards, mesh=grid, in_specs=in_specs, out_specs=out_specs, check_vma=False)
```

```python
import math

import jax
import jax.numpy as jnp
from jax import lax
from jax.sharding import Mesh, PartitionSpec as P

HEADS = 64
KV_HEADS = 4
CAP = 2
EPSILON = 1e-06
THETA = 1000000.0

PLANE = ("y", "core")
EXPERT = ("z", "y", "core")
BF = jnp.bfloat16
F32 = jnp.float32


def rms_rows(values):
    return values * lax.rsqrt(jnp.mean(values * values, axis=-1, keepdims=True) + EPSILON)


def rotate(values, cosine, sine):
    half = values.shape[-1] // 2
    first = values[..., :half]
    second = values[..., half:]
    return jnp.concatenate(
        [first * cosine - second * sine, second * cosine + first * sine], axis=-1
    )


def layout(seq_lengths, seq_offsets, places):
    bounds = jnp.cumsum(seq_lengths)
    starts = bounds - seq_lengths
    segment = jnp.sum((places[:, None] >= bounds[None, :-1]).astype(jnp.int32), axis=1)
    member = segment[:, None] == jnp.arange(seq_lengths.shape[0], dtype=jnp.int32)[None, :]
    begin = jnp.sum(jnp.where(member, starts[None, :], 0), axis=1)
    offset = jnp.sum(jnp.where(member, seq_offsets[None, :], 0), axis=1)
    return (segment, offset + places - begin)


def angles_for(position, head_dim):
    inverse = THETA ** (-(jnp.arange(head_dim // 2, dtype=F32) * 2.0 / head_dim))
    return position.astype(F32)[:, None] * inverse[None, :]


def exchange(value, axes):
    return lax.all_to_all(value, axes, split_axis=0, concat_axis=0, tiled=True)


def swap(value, axis, mask):
    size = lax.axis_size(axis)
    return lax.ppermute(value, axis, [(i, i ^ mask) for i in range(size)])


def around(value, axis):
    return [value] + [swap(value, axis, k) for k in range(1, lax.axis_size(axis))]


def turn(blocks, place):
    blocks, bit = list(blocks), 1
    while bit < len(blocks):
        flip = (place & bit) != 0
        blocks = [jnp.where(flip, blocks[i ^ bit], blocks[i]) for i in range(len(blocks))]
        bit = bit * 2
    return blocks


def trade(blocks, axis, place):
    mine = turn(blocks, place)
    return [mine[0]] + [swap(mine[k], axis, k) for k in range(1, len(mine))]


def total(blocks):
    return sum(block.astype(F32) for block in blocks[1:]) + blocks[0].astype(F32)


def shards(
    hidden_in,
    w_query,
    w_keyvalue,
    w_out,
    key_gain,
    router,
    trainer_gate_up,
    trainer_down,
    expert_ids,
    seq_lengths,
    seq_offsets,
):
    n_seq = lax.axis_size("seq")
    n_z = lax.axis_size("z")
    n_y = lax.axis_size("y")
    n_core = lax.axis_size("core")
    n_plane = n_y * n_core
    n_owner = n_z * n_plane
    x_at = lax.axis_index("seq")
    z_at = lax.axis_index("z")
    y_at = lax.axis_index("y")
    c_at = lax.axis_index("core")
    p_at = y_at * n_core + c_at
    tok_own, width = hidden_in.shape
    head_dim = key_gain.shape[0]
    piece = width // n_plane
    tok_part = tok_own * n_plane
    tok_shard = tok_part * n_z
    kv_dims = w_keyvalue.shape[1] // KV_HEADS
    top_count = expert_ids.shape[1]
    n_experts = router.shape[1]

    with jax.named_scope("weights"):
        query_w = exchange(w_query.reshape(n_plane, piece, head_dim), PLANE)
        kv_w = w_keyvalue.T.reshape(kv_dims, KV_HEADS, n_plane, piece).transpose(1, 2, 0, 3)
        kv_w = jnp.broadcast_to(kv_w[:, None], (KV_HEADS, n_z // KV_HEADS) + kv_w.shape[1:])
        kv_w = exchange(kv_w.reshape(n_owner, kv_dims, piece), EXPERT)
        kv_w = kv_w.reshape(n_owner * kv_dims, piece)
        out_w = w_out.reshape(head_dim, n_y, n_core, piece).transpose(2, 1, 0, 3)
        out_w = turn(trade([out_w[0], out_w[1]], "core", c_at), c_at)
        out_w = jnp.stack(out_w, axis=1)
        out_w = turn(trade([out_w[i] for i in range(n_y)], "y", y_at), y_at)
        out_w = jnp.concatenate(out_w, axis=0).reshape(n_plane * head_dim, piece)

    gate_up_served = exchange(trainer_gate_up, EXPERT)
    gate_up = gate_up_served.reshape(width, 2, -1)

    with jax.named_scope("tokens"):
        hidden = hidden_in.astype(F32)
        normed_own = rms_rows(hidden).astype(BF)
        cut = normed_own.reshape(tok_own, n_y, n_core, piece).transpose(2, 1, 0, 3)
        cut = jnp.stack(turn(trade([cut[0], cut[1]], "core", c_at), c_at), axis=1)
        cut = turn(trade([cut[i] for i in range(n_y)], "y", y_at), y_at)
        cut = jnp.stack(cut).reshape(tok_part, piece)
        pieces = jnp.concatenate(around(cut, "z"), axis=0)

    with jax.named_scope("projections"):
        query_part = jnp.einsum("tp,hpd->thd", pieces, query_w, preferred_element_type=F32)
        kv_part = lax.dot_general(
            pieces, kv_w, (((1,), (1,)), ((), ())), preferred_element_type=F32
        )
        parts = jnp.concatenate([query_part.reshape(tok_shard, -1), kv_part], axis=1).astype(BF)
        parts = parts.reshape(n_y, n_core, tok_part, -1)
        parts = total(trade([parts[:, 0], parts[:, 1]], "core", c_at)).astype(BF)
        query_cols = n_plane * head_dim
        kv_all = [parts[i, :, query_cols:] for i in range(n_y)]
        mine = turn([parts[i, :, :query_cols] for i in range(n_y)], y_at)
        mine = [jnp.concatenate([block_of] + kv_all, axis=1) for block_of in mine]
        sums = total([mine[0]] + [swap(mine[k], "y", k) for k in range(1, n_y)])
        query_full = sums[:, :query_cols].reshape(tok_part, n_plane, head_dim)
        kv_near = sums[:, query_cols:].reshape(tok_part, n_y, 2 * head_dim)
        kv_near = kv_near.transpose(1, 0, 2).astype(BF)

    inside = jnp.arange(tok_part, dtype=jnp.int32)

    def turns(begin):
        where = begin[..., None] + inside
        seg, position = layout(seq_lengths, seq_offsets, where.reshape(-1))
        angles = angles_for(position, head_dim).reshape(where.shape + (-1,))
        return where.reshape(-1), seg, jnp.cos(angles), jnp.sin(angles)

    rows_y = jnp.arange(n_y, dtype=jnp.int32)
    begin_y = x_at * tok_shard + (z_at ^ (rows_y * n_core + c_at)) * tok_part
    unused, unused, cosine_y, sine_y = turns(begin_y)
    begin = x_at * tok_shard + (z_at ^ p_at) * tok_part
    places, segment, cosine, sine = turns(begin)

    with jax.named_scope("keys"):
        key_near = rms_rows(kv_near[:, :, :head_dim].astype(F32)) * key_gain
        key_near = rotate(key_near, cosine_y, sine_y).astype(BF)
        kv_near = jnp.concatenate([key_near, kv_near[:, :, head_dim:]], axis=2)
        kv_mine = lax.dynamic_index_in_dim(kv_near, y_at, 0, keepdims=False)
        near = jnp.stack(around(kv_near, "seq"))
        near, out_w = lax.optimization_barrier((near, out_w))
        near = jnp.stack(around(near, "core"))
        near = near.reshape(n_core * n_seq * n_y * tok_part, 2 * head_dim)
        keys, values = near[:, :head_dim], near[:, head_dim:]
        rel = jnp.arange(n_plane * n_seq, dtype=jnp.int32)
        rel_c, rel_x, row_y = rel // (n_y * n_seq), rel // n_y % n_seq, rel % n_y
        begins = (x_at ^ rel_x) * tok_shard
        begins = begins + (z_at ^ (row_y * n_core + (c_at ^ rel_c))) * tok_part
        key_places = (begins[:, None] + inside[None, :]).reshape(-1)

    with jax.named_scope("attention"):
        queries = rotate(rms_rows(query_full), cosine[:, None], sine[:, None]).astype(BF)
        key_segments, unused = layout(seq_lengths, seq_offsets, key_places)
        scores = jnp.einsum("qhd,kd->qhk", queries, keys, preferred_element_type=F32)
        allowed = (segment[:, None] == key_segments[None, :]) & (
            key_places[None, :] <= places[:, None]
        )
        weights = jnp.where(
            allowed[:, None, :], jnp.exp(scores * (1.0 / math.sqrt(head_dim))), 0.0
        )
        numerator = jnp.einsum(
            "qhk,kd->qhd", weights.astype(BF), values, preferred_element_type=F32
        )
        context = (numerator / jnp.sum(weights, axis=2)[..., None]).astype(BF)

    with jax.named_scope("output"):
        context = context.reshape(tok_part, n_plane * head_dim)
        context = jnp.stack(around(context, "y"))
        context = jnp.stack(around(context, "core"))
        context = context.reshape(tok_shard, n_plane * head_dim)
        out_part = jnp.dot(context, out_w, preferred_element_type=F32).astype(BF)
        out_part = out_part.reshape(n_core, n_y, tok_part, piece)
        out_part = jnp.stack(turn([out_part[0], out_part[1]], c_at), axis=1)
        out_part = turn([out_part[i] for i in range(n_y)], y_at)
        out_part = jnp.stack(out_part).reshape(n_plane, tok_part, piece)
        shares = [out_part[0]] + [swap(out_part[k], "z", k) for k in range(1, n_z)]
        own = total(shares).astype(BF).reshape(n_y, n_core, tok_own, piece)
        own = jnp.stack(turn(trade([own[:, 0], own[:, 1]], "core", c_at), c_at), axis=1)
        own = turn(trade([own[i] for i in range(n_y)], "y", y_at), y_at)
        own = jnp.stack(own).reshape(n_plane, tok_own, piece).transpose(1, 0, 2)
        resid = (hidden + own.reshape(tok_own, width).astype(F32)).astype(BF)
        resid_wide = resid.astype(F32)
        normed = rms_rows(resid_wide).astype(BF)

    normed, gate_up = lax.optimization_barrier((normed, gate_up))

    def placing_of(ids):
        picked = ids[:, :, None] == jnp.arange(n_experts, dtype=jnp.int32)[None, None, :]
        used = jnp.any(picked, axis=1)
        earlier = jnp.cumsum(used.astype(jnp.int32), axis=0) - used.astype(jnp.int32)
        return picked, used[:, :, None] & (
            earlier[:, :, None] == jnp.arange(CAP, dtype=jnp.int32)[None, None, :]
        )

    with jax.named_scope("dispatch"):
        picked, placing = placing_of(expert_ids)
        dispatch_matrix = placing.reshape(tok_own, n_experts * CAP).T.astype(BF)
        send_buffer = jnp.dot(dispatch_matrix, normed, preferred_element_type=F32).astype(BF)
        cache = kv_mine.T.reshape(n_owner, CAP, kv_dims * tok_part // CAP)
        send_buffer = send_buffer.reshape(n_experts, CAP, width)
        arrived = exchange(jnp.concatenate([send_buffer, cache], axis=2), EXPERT)
        cache = arrived[:, :, width:].reshape(n_z, n_plane, kv_dims, tok_part)
        arrived = arrived[:, :, :width].reshape(n_owner * CAP, width)
        arrived, trainer_down = lax.optimization_barrier((arrived, trainer_down))
        step = n_z // KV_HEADS
        cache = jnp.stack(
            [
                jnp.stack([cache[step * k, t ^ (step * k)] for t in range(n_plane)], axis=1)
                for k in range(KV_HEADS)
            ],
            axis=1,
        )
        kv_cache = cache.reshape(kv_dims * KV_HEADS, tok_shard)
        half = arrived.shape[0] // 2
        near_rows, far_rows = swap(arrived, "seq", 1), swap(arrived, "seq", 3)
        top_rows, low_rows = swap(far_rows[:half], "seq", 1), swap(near_rows[half:], "seq", 3)
        expert_rows = [arrived, near_rows, jnp.concatenate([top_rows, low_rows], axis=0), far_rows]
        logits = jnp.dot(normed, router, preferred_element_type=F32)
        chosen = jnp.sum(jnp.where(picked, logits[:, None, :], 0.0), axis=2)
        gates = jax.nn.softmax(chosen, axis=1)

    with jax.named_scope("experts"):
        down_served = exchange(trainer_down, EXPERT)
        down = down_served.reshape(n_seq, -1, trainer_down.shape[2])
        down = turn([down[i] for i in range(n_seq)], x_at)

        def act_of(rows):
            both = jnp.einsum("rd,dgf->grf", rows, gate_up, preferred_element_type=F32)
            return (jax.nn.silu(both[0]) * both[1]).astype(BF)

        act = jnp.concatenate([act_of(rows) for rows in expert_rows], axis=0)
        gates_high = gates.astype(BF)
        gates_low = (gates - gates_high.astype(F32)).astype(BF)
        gate_block = jnp.concatenate([gates_high, gates_low], axis=0)
        ids_block = jnp.concatenate([expert_ids, expert_ids], axis=0).astype(BF)
        gate_pad = jnp.zeros((2 * tok_own, act.shape[1] - 2 * top_count), BF)
        gate_block = jnp.concatenate([gate_block, ids_block, gate_pad], axis=1)
        n_rows = act.shape[0]
        wide = around(jnp.concatenate([act, gate_block], axis=0), "seq")
        blocks = [piece_of[n_rows:].astype(F32) for piece_of in wide]
        gates_all = jnp.stack([b[:tok_own, :top_count] + b[tok_own:, :top_count] for b in blocks])
        ids_all = jnp.stack([b[:tok_own, top_count : 2 * top_count] for b in blocks])
        ids_all = ids_all.astype(jnp.int32)
        shape = (n_seq, n_rows // n_seq, -1)
        outputs = 0.0
        for k in range(n_seq):
            from_k = wide[k][:n_rows].reshape(shape)
            from_k = jnp.concatenate([from_k[j ^ k] for j in range(n_seq)], axis=0)
            outputs = outputs + jnp.dot(from_k, down[k], preferred_element_type=F32)
        outputs = outputs.astype(BF)

    with jax.named_scope("combine"):
        columns = outputs.shape[1]
        outputs = outputs.reshape(n_seq, n_owner, CAP, columns).transpose(1, 0, 2, 3)
        returned = exchange(outputs.reshape(n_owner, n_seq * CAP, columns), EXPERT)
        returned = returned.reshape(n_owner, n_seq, CAP, columns)
        picked_all, placing_all = jax.vmap(placing_of)(ids_all)
        gate_of = jnp.sum(jnp.where(picked_all, gates_all[:, :, :, None], 0.0), axis=2)
        combine_matrix = jnp.where(placing_all, gate_of[:, :, :, None], 0.0)
        combine_high = combine_matrix.astype(BF)
        combine_low = (combine_matrix - combine_high.astype(F32)).astype(BF)
        rows = returned.transpose(1, 0, 2, 3).reshape(n_seq, n_owner * CAP, columns)
        combine_both = jnp.concatenate([combine_high, combine_low], axis=1)
        moe = jnp.einsum(
            "xts,xsc->xtc",
            combine_both.reshape(n_seq, 2 * tok_own, n_experts * CAP),
            rows,
            preferred_element_type=F32,
        )
        moe = (moe[:, :tok_own] + moe[:, tok_own:]).astype(BF)
        moe = [moe[0]] + [swap(moe[k], "seq", k) for k in range(1, n_seq)]
        moe = jnp.concatenate(turn(moe, x_at), axis=1)
        mixed = (resid_wide + moe.astype(F32)).astype(BF)
    return (mixed, kv_cache)


def solution(mesh):
    n_seq, n_owner = mesh.devices.shape
    grid = Mesh(mesh.devices.reshape(n_seq, n_owner // 8, 4, 2), ("seq", "z", "y", "core"))
    in_specs = (
        P(("seq",) + EXPERT, None),
        P(None, EXPERT),
        P(None, EXPERT),
        P(EXPERT, None),
        P(),
        P(),
        P(None, EXPERT, None, "seq"),
        P(None, EXPERT, "seq"),
        P(("seq",) + EXPERT, None),
        P(),
        P(),
    )
    out_specs = (P(("seq",) + EXPERT, None), P(EXPERT, "seq"))
    return jax.shard_map(shards, mesh=grid, in_specs=in_specs, out_specs=out_specs, check_vma=False)
```

```python
import math

import jax
import jax.numpy as jnp
from jax import lax
from jax.sharding import Mesh, PartitionSpec as P

HEADS = 64
KV_HEADS = 4
CAP = 2
EPSILON = 1e-06
THETA = 1000000.0

PLANE = ("y", "core")
EXPERT = ("z", "y", "core")
BF = jnp.bfloat16
F32 = jnp.float32


def rms_rows(values):
    return values * lax.rsqrt(jnp.mean(values * values, axis=-1, keepdims=True) + EPSILON)


def rotate(values, cosine, sine):
    half = values.shape[-1] // 2
    first = values[..., :half]
    second = values[..., half:]
    return jnp.concatenate(
        [first * cosine - second * sine, second * cosine + first * sine], axis=-1
    )


def layout(seq_lengths, seq_offsets, places):
    bounds = jnp.cumsum(seq_lengths)
    starts = bounds - seq_lengths
    segment = jnp.sum((places[:, None] >= bounds[None, :-1]).astype(jnp.int32), axis=1)
    member = segment[:, None] == jnp.arange(seq_lengths.shape[0], dtype=jnp.int32)[None, :]
    begin = jnp.sum(jnp.where(member, starts[None, :], 0), axis=1)
    offset = jnp.sum(jnp.where(member, seq_offsets[None, :], 0), axis=1)
    return (segment, offset + places - begin)


def angles_for(position, head_dim):
    inverse = THETA ** (-(jnp.arange(head_dim // 2, dtype=F32) * 2.0 / head_dim))
    return position.astype(F32)[:, None] * inverse[None, :]


def exchange(value, axes):
    return lax.all_to_all(value, axes, split_axis=0, concat_axis=0, tiled=True)


def swap(value, axis, mask):
    size = lax.axis_size(axis)
    return lax.ppermute(value, axis, [(i, i ^ mask) for i in range(size)])


def around(value, axis):
    return [value] + [swap(value, axis, k) for k in range(1, lax.axis_size(axis))]


def turn(blocks, place):
    blocks, bit = list(blocks), 1
    while bit < len(blocks):
        flip = (place & bit) != 0
        blocks = [jnp.where(flip, blocks[i ^ bit], blocks[i]) for i in range(len(blocks))]
        bit = bit * 2
    return blocks


def trade(blocks, axis, place):
    mine = turn(blocks, place)
    return [mine[0]] + [swap(mine[k], axis, k) for k in range(1, len(mine))]


def total(blocks):
    return sum(block.astype(F32) for block in blocks[1:]) + blocks[0].astype(F32)


def shards(
    hidden_in,
    w_query,
    w_keyvalue,
    w_out,
    key_gain,
    router,
    trainer_gate_up,
    trainer_down,
    expert_ids,
    seq_lengths,
    seq_offsets,
):
    n_seq = lax.axis_size("seq")
    n_z = lax.axis_size("z")
    n_y = lax.axis_size("y")
    n_core = lax.axis_size("core")
    n_plane = n_y * n_core
    n_owner = n_z * n_plane
    x_at = lax.axis_index("seq")
    z_at = lax.axis_index("z")
    y_at = lax.axis_index("y")
    c_at = lax.axis_index("core")
    p_at = y_at * n_core + c_at
    tok_own, width = hidden_in.shape
    head_dim = key_gain.shape[0]
    piece = width // n_plane
    tok_part = tok_own * n_plane
    tok_shard = tok_part * n_z
    kv_dims = w_keyvalue.shape[1] // KV_HEADS
    top_count = expert_ids.shape[1]
    n_experts = router.shape[1]

    with jax.named_scope("weights"):
        query_w = exchange(w_query.reshape(n_plane, piece, head_dim), PLANE)
        kv_w = w_keyvalue.T.reshape(kv_dims, KV_HEADS, n_plane, piece).transpose(1, 2, 0, 3)
        kv_w = jnp.broadcast_to(kv_w[:, None], (KV_HEADS, n_z // KV_HEADS) + kv_w.shape[1:])
        kv_w = exchange(kv_w.reshape(n_owner, kv_dims, piece), EXPERT)
        kv_w = kv_w.reshape(n_owner * kv_dims, piece)
        out_w = w_out.reshape(head_dim, n_y, n_core, piece).transpose(2, 1, 0, 3)
        out_w = turn(trade([out_w[0], out_w[1]], "core", c_at), c_at)
        out_w = jnp.stack(out_w, axis=1)

    gate_up_served = exchange(trainer_gate_up, EXPERT)
    gate_up = gate_up_served.reshape(width, 2, -1)

    with jax.named_scope("tokens"):
        hidden = hidden_in.astype(F32)
        normed_own = rms_rows(hidden).astype(BF)
        cut = normed_own.reshape(tok_own, n_y, n_core, piece).transpose(2, 1, 0, 3)
        cut = jnp.stack(turn(trade([cut[0], cut[1]], "core", c_at), c_at), axis=1)
        cut = turn(trade([cut[i] for i in range(n_y)], "y", y_at), y_at)
        cut = jnp.stack(cut).reshape(tok_part, piece)
        pieces = jnp.concatenate(around(cut, "z"), axis=0)

    with jax.named_scope("projections"):
        query_part = jnp.einsum("tp,hpd->thd", pieces, query_w, preferred_element_type=F32)
        kv_part = lax.dot_general(
            pieces, kv_w, (((1,), (1,)), ((), ())), preferred_element_type=F32
        )
        parts = jnp.concatenate([query_part.reshape(tok_shard, -1), kv_part], axis=1).astype(BF)
        parts = parts.reshape(n_y, n_core, tok_part, -1)
        parts = total(trade([parts[:, 0], parts[:, 1]], "core", c_at)).astype(BF)
        query_cols = n_plane * head_dim
        kv_all = [parts[i, :, query_cols:] for i in range(n_y)]
        mine = turn([parts[i, :, :query_cols] for i in range(n_y)], y_at)
        mine = [jnp.concatenate([block_of] + kv_all, axis=1) for block_of in mine]
        sums = total([mine[0]] + [swap(mine[k], "y", k) for k in range(1, n_y)])
        query_full = sums[:, :query_cols].reshape(tok_part, n_plane, head_dim)
        kv_near = sums[:, query_cols:].reshape(tok_part, n_y, 2 * head_dim)
        kv_near = kv_near.transpose(1, 0, 2).astype(BF)

    inside = jnp.arange(tok_part, dtype=jnp.int32)

    def turns(begin):
        where = begin[..., None] + inside
        seg, position = layout(seq_lengths, seq_offsets, where.reshape(-1))
        angles = angles_for(position, head_dim).reshape(where.shape + (-1,))
        return where.reshape(-1), seg, jnp.cos(angles), jnp.sin(angles)

    rows_y = jnp.arange(n_y, dtype=jnp.int32)
    begin_y = x_at * tok_shard + (z_at ^ (rows_y * n_core + c_at)) * tok_part
    unused, unused, cosine_y, sine_y = turns(begin_y)
    begin = x_at * tok_shard + (z_at ^ p_at) * tok_part
    places, segment, cosine, sine = turns(begin)

    with jax.named_scope("keys"):
        key_near = rms_rows(kv_near[:, :, :head_dim].astype(F32)) * key_gain
        key_near = rotate(key_near, cosine_y, sine_y).astype(BF)
        kv_near = jnp.concatenate([key_near, kv_near[:, :, head_dim:]], axis=2)
        kv_mine = lax.dynamic_index_in_dim(kv_near, y_at, 0, keepdims=False)
        near = jnp.stack(around(kv_near, "seq"))
        near = jnp.stack(around(near, "core"))
        near = near.reshape(n_core * n_seq * n_y * tok_part, 2 * head_dim)
        keys, values = near[:, :head_dim], near[:, head_dim:]
        rel = jnp.arange(n_plane * n_seq, dtype=jnp.int32)
        rel_c, rel_x, row_y = rel // (n_y * n_seq), rel // n_y % n_seq, rel % n_y
        begins = (x_at ^ rel_x) * tok_shard
        begins = begins + (z_at ^ (row_y * n_core + (c_at ^ rel_c))) * tok_part
        key_places = (begins[:, None] + inside[None, :]).reshape(-1)

    with jax.named_scope("attention"):
        queries = rotate(rms_rows(query_full), cosine[:, None], sine[:, None]).astype(BF)
        key_segments, unused = layout(seq_lengths, seq_offsets, key_places)
        scores = jnp.einsum("qhd,kd->qhk", queries, keys, preferred_element_type=F32)
        allowed = (segment[:, None] == key_segments[None, :]) & (
            key_places[None, :] <= places[:, None]
        )
        weights = jnp.where(
            allowed[:, None, :], jnp.exp(scores * (1.0 / math.sqrt(head_dim))), 0.0
        )
        numerator = jnp.einsum(
            "qhk,kd->qhd", weights.astype(BF), values, preferred_element_type=F32
        )
        context = (numerator / jnp.sum(weights, axis=2)[..., None]).astype(BF)

    with jax.named_scope("output"):
        context = context.reshape(tok_part, n_plane * head_dim)
        context = jnp.stack(around(context, "y"))
        context, out_w = lax.optimization_barrier((context, out_w))
        out_w = turn(trade([out_w[i] for i in range(n_y)], "y", y_at), y_at)
        out_w = jnp.concatenate(out_w, axis=0).reshape(n_plane * head_dim, piece)
        context = jnp.stack(around(context, "core"))
        context = context.reshape(tok_shard, n_plane * head_dim)
        out_part = jnp.dot(context, out_w, preferred_element_type=F32).astype(BF)
        out_part = out_part.reshape(n_core, n_y, tok_part, piece)
        out_part = jnp.stack(turn([out_part[0], out_part[1]], c_at), axis=1)
        out_part = turn([out_part[i] for i in range(n_y)], y_at)
        out_part = jnp.stack(out_part).reshape(n_plane, tok_part, piece)
        shares = [out_part[0]] + [swap(out_part[k], "z", k) for k in range(1, n_z)]
        own = total(shares).astype(BF).reshape(n_y, n_core, tok_own, piece)
        own = jnp.stack(turn(trade([own[:, 0], own[:, 1]], "core", c_at), c_at), axis=1)
        own = turn(trade([own[i] for i in range(n_y)], "y", y_at), y_at)
        own = jnp.stack(own).reshape(n_plane, tok_own, piece).transpose(1, 0, 2)
        resid = (hidden + own.reshape(tok_own, width).astype(F32)).astype(BF)
        resid_wide = resid.astype(F32)
        normed = rms_rows(resid_wide).astype(BF)

    normed, gate_up = lax.optimization_barrier((normed, gate_up))

    def placing_of(ids):
        picked = ids[:, :, None] == jnp.arange(n_experts, dtype=jnp.int32)[None, None, :]
        used = jnp.any(picked, axis=1)
        earlier = jnp.cumsum(used.astype(jnp.int32), axis=0) - used.astype(jnp.int32)
        return picked, used[:, :, None] & (
            earlier[:, :, None] == jnp.arange(CAP, dtype=jnp.int32)[None, None, :]
        )

    with jax.named_scope("dispatch"):
        picked, placing = placing_of(expert_ids)
        dispatch_matrix = placing.reshape(tok_own, n_experts * CAP).T.astype(BF)
        send_buffer = jnp.dot(dispatch_matrix, normed, preferred_element_type=F32).astype(BF)
        cache = kv_mine.T.reshape(n_owner, CAP, kv_dims * tok_part // CAP)
        send_buffer = send_buffer.reshape(n_experts, CAP, width)
        arrived = exchange(jnp.concatenate([send_buffer, cache], axis=2), EXPERT)
        cache = arrived[:, :, width:].reshape(n_z, n_plane, kv_dims, tok_part)
        arrived = arrived[:, :, :width].reshape(n_owner * CAP, width)
        arrived, trainer_down = lax.optimization_barrier((arrived, trainer_down))
        step = n_z // KV_HEADS
        cache = jnp.stack(
            [
                jnp.stack([cache[step * k, t ^ (step * k)] for t in range(n_plane)], axis=1)
                for k in range(KV_HEADS)
            ],
            axis=1,
        )
        kv_cache = cache.reshape(kv_dims * KV_HEADS, tok_shard)
        half = arrived.shape[0] // 2
        near_rows, far_rows = swap(arrived, "seq", 1), swap(arrived, "seq", 3)
        top_rows, low_rows = swap(far_rows[:half], "seq", 1), swap(near_rows[half:], "seq", 3)
        expert_rows = [arrived, near_rows, jnp.concatenate([top_rows, low_rows], axis=0), far_rows]
        logits = jnp.dot(normed, router, preferred_element_type=F32)
        chosen = jnp.sum(jnp.where(picked, logits[:, None, :], 0.0), axis=2)
        gates = jax.nn.softmax(chosen, axis=1)

    with jax.named_scope("experts"):
        down_served = exchange(trainer_down, EXPERT)
        down = down_served.reshape(n_seq, -1, trainer_down.shape[2])
        down = turn([down[i] for i in range(n_seq)], x_at)

        def act_of(rows):
            both = jnp.einsum("rd,dgf->grf", rows, gate_up, preferred_element_type=F32)
            return (jax.nn.silu(both[0]) * both[1]).astype(BF)

        act = jnp.concatenate([act_of(rows) for rows in expert_rows], axis=0)
        gates_high = gates.astype(BF)
        gates_low = (gates - gates_high.astype(F32)).astype(BF)
        gate_block = jnp.concatenate([gates_high, gates_low], axis=0)
        ids_block = jnp.concatenate([expert_ids, expert_ids], axis=0).astype(BF)
        gate_pad = jnp.zeros((2 * tok_own, act.shape[1] - 2 * top_count), BF)
        gate_block = jnp.concatenate([gate_block, ids_block, gate_pad], axis=1)
        n_rows = act.shape[0]
        wide = around(jnp.concatenate([act, gate_block], axis=0), "seq")
        blocks = [piece_of[n_rows:].astype(F32) for piece_of in wide]
        gates_all = jnp.stack([b[:tok_own, :top_count] + b[tok_own:, :top_count] for b in blocks])
        ids_all = jnp.stack([b[:tok_own, top_count : 2 * top_count] for b in blocks])
        ids_all = ids_all.astype(jnp.int32)
        shape = (n_seq, n_rows // n_seq, -1)
        outputs = 0.0
        for k in range(n_seq):
            from_k = wide[k][:n_rows].reshape(shape)
            from_k = jnp.concatenate([from_k[j ^ k] for j in range(n_seq)], axis=0)
            outputs = outputs + jnp.dot(from_k, down[k], preferred_element_type=F32)
        outputs = outputs.astype(BF)

    with jax.named_scope("combine"):
        columns = outputs.shape[1]
        outputs = outputs.reshape(n_seq, n_owner, CAP, columns).transpose(1, 0, 2, 3)
        returned = exchange(outputs.reshape(n_owner, n_seq * CAP, columns), EXPERT)
        returned = returned.reshape(n_owner, n_seq, CAP, columns)
        picked_all, placing_all = jax.vmap(placing_of)(ids_all)
        gate_of = jnp.sum(jnp.where(picked_all, gates_all[:, :, :, None], 0.0), axis=2)
        combine_matrix = jnp.where(placing_all, gate_of[:, :, :, None], 0.0)
        combine_high = combine_matrix.astype(BF)
        combine_low = (combine_matrix - combine_high.astype(F32)).astype(BF)
        rows = returned.transpose(1, 0, 2, 3).reshape(n_seq, n_owner * CAP, columns)
        combine_both = jnp.concatenate([combine_high, combine_low], axis=1)
        moe = jnp.einsum(
            "xts,xsc->xtc",
            combine_both.reshape(n_seq, 2 * tok_own, n_experts * CAP),
            rows,
            preferred_element_type=F32,
        )
        moe = (moe[:, :tok_own] + moe[:, tok_own:]).astype(BF)
        moe = [moe[0]] + [swap(moe[k], "seq", k) for k in range(1, n_seq)]
        moe = jnp.concatenate(turn(moe, x_at), axis=1)
        mixed = (resid_wide + moe.astype(F32)).astype(BF)
    return (mixed, kv_cache)


def solution(mesh):
    n_seq, n_owner = mesh.devices.shape
    grid = Mesh(mesh.devices.reshape(n_seq, n_owner // 8, 4, 2), ("seq", "z", "y", "core"))
    in_specs = (
        P(("seq",) + EXPERT, None),
        P(None, EXPERT),
        P(None, EXPERT),
        P(EXPERT, None),
        P(),
        P(),
        P(None, EXPERT, None, "seq"),
        P(None, EXPERT, "seq"),
        P(("seq",) + EXPERT, None),
        P(),
        P(),
    )
    out_specs = (P(("seq",) + EXPERT, None), P(EXPERT, "seq"))
    return jax.shard_map(shards, mesh=grid, in_specs=in_specs, out_specs=out_specs, check_vma=False)
```
